512 devices in a mesh: slab: 16 (over y, x), sta: 32 (over z, core).
Axes of the slice: x: 4, y: 4, z: 16, core: 2. Of those that a mesh axis runs over, the one named last changes fastest.
Arguments:
- station_place: float32 [128, 2], P('sta'), may hold values from 0 to 1
- station_height: float32 [128], P('sta'), may hold values from 2 to 8
- cell_weight: float32 [256, 256, 64], P('slab'), may hold values from 0.5 to 2
- kept: int32 [16, 128, 16], P('slab', 'sta'), may hold values from 0 to 2047, as said below
- dest: int32 [16, 128, 16, 1], P('slab', 'sta'), may hold values from 0 to 31; in each aligned block of 64 rows (0 to 63, 64 to 127, ..., all dimensions but the last counted through in order) at most 6 rows name the same one
Outputs:
- owned_blocks: float32 [16, 32, 32, 6, 128], P('slab', 'sta')
The draws below stay inside these ranges and needn't reach their ends.
Inputs may be any that keep to these rules, and one draw needn't show every extreme that they name: `dest`: in the rows of one device (aligned blocks of 64 rows, in order), each owner is named by at most 6 rows, a bound that some block reaches. Let a = k // (256 / (2 * 16)) for a kept id k, and let x-slab p hold x from p * 256 / 16 on, 256 / 16 of them. When a >= 16, the cells on which row a of H(256) is nonzero lie in one x-slab. Among the 64 ids of one y-slab and one index of sta, at most 8 ids with a >= 16 touch any one x-slab, and some x-slab is touched by exactly 8.
All inputs are finite; a program needn't handle non-finite values.
Results may differ from the reference program's by a relative error of at most 0.0003.
Values sent between devices are 32-bit elements; how exact they have to be, the bound alone decides.
No kernel may reach another device: no remote copies, remote signals or barrier semaphores. Data moves between devices by JAX's collectives and lax.ppermute only.
A program may use at most 64 MiB of HBM per device.

```python
import math
import jax
import jax.numpy as jnp
import numpy as np
from jax import lax

NX = 256
NY = 256
NZ = 64
STA_DEV = 4
KEEP = 16
STATIONS = 128
CAP = 6
N_SLAB = 16
N_STA = 32


def fine_row(slab, chosen):
    x_local = NX // N_SLAB
    result = jnp.zeros_like(chosen)
    base = 0
    width = 2
    while width <= x_local:
        count = x_local // width
        inside = (chosen >= base) & (chosen < base + count)
        result = jnp.where(inside, NX // width + slab * count + chosen - base, result)
        base = base + count
        width = width * 2
    return result


def draw_kept(key, part):
    rows = STA_DEV * KEEP
    half = NY // N_SLAB // 2
    x_local = NX // N_SLAB
    limit = max(2, 2 * rows // N_SLAB)
    classes = N_SLAB + 1

    def one_group(sub):
        keys = jax.random.split(sub, 6)
        full_slab = jax.random.randint(keys[0], (), 0, N_SLAB)
        shuffled = jax.random.permutation(keys[1], classes * limit)
        class_of = (shuffled // limit).astype(jnp.int32)
        score = jnp.where(class_of == full_slab, 0, 1 + jnp.arange(classes * limit, dtype=jnp.int32))
        ordered = class_of[jnp.argsort(score, stable=True)]
        taken = jax.random.permutation(keys[2], ordered[:rows])
        chosen = jax.random.randint(keys[3], (rows,), 0, x_local - 1)
        fine = fine_row(jnp.minimum(taken, N_SLAB - 1), chosen)
        coarse = jax.random.randint(keys[4], (rows,), 0, N_SLAB)
        xrows = jnp.where(taken == N_SLAB, coarse, fine)
        pairs = jax.random.randint(keys[5], (rows,), 0, half)
        return (xrows * half + pairs).astype(jnp.int32)
    groups = jax.random.split(jax.random.fold_in(key, 71), N_SLAB * N_STA)
    table = jax.vmap(one_group)(groups)
    return table.reshape(N_SLAB, N_STA * STA_DEV, KEEP)


def levels(own_key, extent, pieces, least, high):
    def one(dim, parts):
        draws = jax.random.uniform(jax.random.fold_in(jax.random.fold_in(own_key, 6), dim), (parts,), jnp.float32, least / len(pieces), high / len(pieces))
        return jnp.repeat(jnp.exp(draws), extent[dim] // parts).reshape((-1,) + (1,) * (len(extent) - dim - 1))

    level = one(*pieces[0])
    for cut in pieces[1:]:
        level = level * one(*cut)
    return level


def shared_out(key, own, number, rows, number_of, top, reach, skew):
    ranking = jax.random.permutation(key, number_of)
    packed, common = load_shares(number_of, rows * top, reach, skew, True), load_shares(number_of, rows * top, reach, skew, False)
    places = jnp.arange(number_of)

    def named(lengths, turn):
        used = int((lengths > 0).sum())
        fixed = max(1, used // 4)
        passed = fixed + (places - fixed + turn * (used - fixed)) % max(1, number_of - fixed)
        return jnp.zeros((number_of,), jnp.int32).at[ranking[jnp.where(places < fixed, places, passed)]].set(jnp.asarray(lengths, jnp.int32))

    lengths = jnp.where(number % 4 == 0, named(packed, number // 4), named(common, number - number // 4 - 1))
    mixed = jax.random.permutation(jax.random.fold_in(own, 3), number_of)
    donor, sink = mixed[0:number_of // 2 * 2:2], mixed[1:number_of // 2 * 2:2]
    margin = jnp.minimum(lengths[donor] - 1, reach - lengths[sink]) // 2
    margin = jnp.where((donor == ranking[0]) | (sink == ranking[0]) | (lengths[sink] == 0), 0, jnp.maximum(margin, 0))
    passed = jax.random.randint(jax.random.fold_in(own, 4), (number_of // 2,), 0, 1 << 20) % (margin + 1)
    lengths = lengths.at[donor].add(-passed).at[sink].add(passed)
    members = jnp.searchsorted(jnp.cumsum(lengths), jnp.arange(rows * top), side="right").astype(jnp.int32)
    grid = members.reshape(top, rows).T
    grid = grid[jax.random.permutation(jax.random.fold_in(own, 1), rows)]
    turn = jax.random.randint(jax.random.fold_in(own, 2), (rows, 1), 0, top)
    return jnp.take_along_axis(grid, (jnp.arange(top)[None, :] + turn) % top, axis=1)


def load_shares(number_of, total, most, skew, full):
    weights = [(1 << 20) // math.isqrt(standing ** skew) + 1 for standing in range(1, number_of + 1)]
    largest = most if full else min(most, max(-(-total // number_of), total * weights[0] // sum(weights)))
    least = 1 if total - largest >= number_of - 1 else 0
    holding, surplus = [largest] + [least] * (number_of - 1), total - largest - least * (number_of - 1)
    while surplus > 0:
        free = [i for i in range(1, number_of) if holding[i] < largest] or [i for i in range(1, number_of) if holding[i] < most]
        pool, budget = sum([weights[i] for i in free]), surplus
        for i in free:
            more = min(most - holding[i], max(1, budget * weights[i] // pool), surplus)
            holding[i] = holding[i] + more
            surplus = surplus - more
    return np.array(holding)


def setup_inputs(seed: int = 0) -> dict:
    streams_of = jax.random.split(jax.random.key(seed), 6)
    station_place = jnp.clip(1.0 * jax.random.uniform(streams_of[0], (STATIONS, 2), jnp.float32) ** levels(streams_of[0], (STATIONS, 2), ((0, 32),), -0.2, 0.2), 0.0, 1.0)
    station_height = jnp.clip(jnp.exp(math.log(8.0) - 1.3862944 * jax.random.uniform(streams_of[1], (STATIONS,), jnp.float32) ** levels(streams_of[1], (STATIONS,), ((0, 32),), -0.2, 0.2)), 2.0, 8.0)
    cell_weight = jnp.clip(jnp.exp(math.log(2.0) - 1.3862944 * jax.random.uniform(streams_of[2], (NX, NY, NZ), jnp.float32) ** levels(streams_of[2], (NX, NY, NZ), ((0, 16),), -0.2, 0.2)), 0.5, 2.0)
    kept = draw_kept(jax.random.fold_in(streams_of[5], 71), 0)
    dest_keys = jax.random.split(jax.random.fold_in(streams_of[4], 1), N_SLAB * STATIONS * KEEP // (STA_DEV * KEEP))
    dest_turns = jax.random.permutation(jax.random.fold_in(streams_of[4], 3), N_SLAB * STATIONS * KEEP // (STA_DEV * KEEP))
    dest = jax.vmap(lambda own, number: shared_out(jax.random.fold_in(streams_of[4], 2), own, number, STA_DEV * KEEP, N_STA, 1, CAP, 2))(dest_keys, dest_turns).reshape((N_SLAB, STATIONS, KEEP, 1))
    return dict(station_place=station_place, station_height=station_height, cell_weight=cell_weight, kept=kept, dest=dest)


kernel_scale = 32.0
root_half = 0.7071067811865476

def haar(order):
    matrix = jnp.eye(order, dtype=jnp.float32)
    rows = jnp.arange(order, dtype=jnp.int32)[:, None]
    cols = jnp.arange(order, dtype=jnp.int32)[None, :]
    active = order
    while active % 2 == 0 and active > 1:
        half = active // 2
        low = (rows < half) & ((cols == 2 * rows) | (cols == 2 * rows + 1))
        upper = (rows >= half) & (rows < active)
        plus = upper & (cols == 2 * (rows - half))
        minus = upper & (cols == 2 * (rows - half) + 1)
        keeps = (rows >= active) & (rows == cols)
        step = (jnp.where(low | plus, root_half, 0.0) - jnp.where(minus, root_half, 0.0) + jnp.where(keeps, 1.0, 0.0)).astype(jnp.float32)
        matrix = jnp.dot(step, matrix, precision=lax.Precision.HIGHEST, preferred_element_type=jnp.float32)
        active = half
    return matrix

def kernel(place, height, weight, xs, nx, ny, nz):
    ys = jnp.arange(ny, dtype=jnp.int32).astype(jnp.float32) + 0.5
    zs = jnp.arange(nz, dtype=jnp.int32).astype(jnp.float32) + 0.5
    east = xs[None, :] - place[:, 0:1] * nx
    north = ys[None, :] - place[:, 1:2] * ny
    depth = zs[None, :] + height[:, None]
    radius = east[:, :, None, None] ** 2 + north[:, None, :, None] ** 2 + depth[:, None, None, :] ** 2
    return kernel_scale * weight[None] * depth[:, None, None, :] / (radius * jnp.sqrt(radius))

def reference(station_place, station_height, cell_weight, kept, dest):
    wx, wy, wz = (haar(NX), haar(NY), haar(NZ))
    half = NY // N_SLAB // 2
    xs = jnp.arange(NX, dtype=jnp.int32).astype(jnp.float32) + 0.5
    slabs = jnp.arange(N_SLAB, dtype=jnp.int32)[:, None]

    def one(item):
        place, height, ids = item
        field = kernel(place[None], height[None], cell_weight, xs, NX, NY, NZ)[0]
        field = jnp.einsum('xyz,cz->xyc', field, wz, precision=lax.Precision.HIGHEST)
        field = jnp.einsum('by,xyc->xbc', wy, field, precision=lax.Precision.HIGHEST)
        paired = field.reshape(NX, NY // 2, 2 * NZ)
        xrow = (ids // half).reshape(-1)
        ypair = (slabs * half + ids % half).reshape(-1)
        gathered = paired[:, ypair, :]
        weights = wx[xrow]
        blocks = jnp.einsum('mx,xmc->mc', weights, gathered, precision=lax.Precision.HIGHEST)
        return blocks.reshape(N_SLAB, KEEP, 2 * NZ)
    blocks = lax.map(one, (station_place, station_height, jnp.transpose(kept, (1, 0, 2))))
    per_row = STA_DEV * KEEP
    values = jnp.transpose(blocks, (1, 0, 2, 3)).reshape(N_SLAB, N_STA, per_row, 2 * NZ)
    owner = dest.reshape(N_SLAB, N_STA, per_row)
    owners = jnp.arange(N_STA, dtype=jnp.int32)
    onehot = (owner[..., None] == owners).astype(jnp.int32)
    slot = lax.optimization_barrier(jnp.sum((jnp.cumsum(onehot, axis=2) - onehot) * onehot, axis=3)).astype(jnp.int32)
    slab_ids = jnp.arange(N_SLAB, dtype=jnp.int32)[:, None, None]
    source = jnp.arange(N_STA, dtype=jnp.int32)[None, :, None]
    result = jnp.zeros((N_SLAB, N_STA, N_STA, CAP, 2 * NZ), jnp.float32)
    return result.at[slab_ids, owner, source, slot].set(values)
```

```python
import functools

import jax
import jax.numpy as jnp
import numpy as np
from jax import lax
from jax.experimental import pallas as pl
from jax.experimental.pallas import tpu as pltpu
from jax.sharding import PartitionSpec as P

SCALE = 32.0
SLABS = 16
OWNERS = 32
STA = 4
KEEP = 16
ROWS = STA * KEEP
XL = 16
NX = 256
NY = 256
NZ = 64
HALF = 8
CAP = 6
FINE = 8
COARSE = STA * HALF
MSG = COARSE + FINE
LANES = 2 * NZ
TABS = STA * XL
MIB = 1 << 20


def signs(order):
    out = np.zeros((order, order), np.float32)
    out[0] = 1
    count = 1
    while count < order:
        width = order // count
        for k in range(count):
            out[count + k, k * width : k * width + width // 2] = 1
            out[count + k, k * width + width // 2 : (k + 1) * width] = -1
        count *= 2
    return out


def constants():
    sy = signs(NY)
    sy = np.concatenate([sy[0::2], sy[1::2]], axis=0)
    sy = np.concatenate([sy, sy], axis=1)
    sz = np.zeros((LANES, LANES), np.float32)
    sz[:NZ, :NZ] = signs(NZ).T
    sz[NZ:, NZ:] = signs(NZ).T
    sz = np.concatenate([sz] * 3, axis=0)
    sx = np.repeat(signs(SLABS), COARSE, axis=1)
    bf = jnp.bfloat16
    return np.asarray(sy, bf), np.asarray(sz, bf), np.asarray(sx, bf)


def slab_pos():
    return lax.axis_index("slab")


def iota(shape, dim):
    return lax.broadcasted_iota(jnp.int32, shape, dim)


def column(tile):
    eye = iota((KEEP, KEEP), 0) == iota((KEEP, KEEP), 1)
    parts = []
    for s in range(STA):
        row = jnp.broadcast_to(tile[s : s + 1, :], (KEEP, KEEP))
        parts.append(jnp.sum(jnp.where(eye, row, 0.0), axis=1, keepdims=True))
    return jnp.concatenate(parts, axis=0)


def turned(col):
    eye = iota((ROWS, ROWS), 0) == iota((ROWS, ROWS), 1)
    wide = jnp.broadcast_to(col, (ROWS, ROWS))
    return jnp.sum(jnp.where(eye, wide, 0.0), axis=0, keepdims=True)


def earlier(col):
    row = turned(col)
    before = iota((ROWS, ROWS), 1) < iota((ROWS, ROWS), 0)
    same = (jnp.broadcast_to(row, (ROWS, ROWS)) == jnp.broadcast_to(col, (ROWS, ROWS))) & before
    return jnp.sum(jnp.where(same, 1.0, 0.0), axis=1, keepdims=True)


def split(x, parts):
    out = []
    for i in range(parts):
        piece = x.astype(jnp.bfloat16)
        out.append(piece)
        if i + 1 < parts:
            x = x - piece.astype(jnp.float32)
    return out


def places_of(k):
    a = lax.shift_right_logical(k, 3)
    pair = k & (HALF - 1)
    xs = jnp.full_like(a, SLABS)
    tab = jnp.full_like(a, XL - 1)
    for least, shift, base in ((16, 0, 14), (32, 1, 12), (64, 2, 8), (128, 3, 0)):
        inside = a >= least
        off = a - least
        xs = jnp.where(inside, lax.shift_right_logical(off, shift), xs)
        tab = jnp.where(inside, base + (off & ((1 << shift) - 1)), tab)
    return a, pair, xs, tab


def station_col():
    return lax.shift_right_logical(iota((ROWS, 1), 0), 4)


def list_kernel(kept_ref, out_ref):
    k = column(kept_ref[...].astype(jnp.float32)).astype(jnp.int32)
    _, pair, xs, tab = places_of(k)
    table = station_col() * XL + tab
    code = (table & 1) * 256 + lax.shift_right_logical(table, 1) * HALF + pair
    rank = earlier(xs.astype(jnp.float32)).astype(jnp.int32)
    key = turned((xs * FINE + rank).astype(jnp.float32)).astype(jnp.int32)
    coderow = turned(code.astype(jnp.float32))
    count = SLABS * FINE
    hit = jnp.broadcast_to(key, (count, ROWS)) == iota((count, ROWS), 0)
    found = jnp.sum(jnp.where(hit, jnp.broadcast_to(coderow, (count, ROWS)) + 1.0, 0.0), axis=1, keepdims=True)
    tile = jnp.broadcast_to(found - 1.0, (count, 128)).astype(jnp.int32)
    out_ref[...] = tile.reshape(SLABS, FINE, 128)


def table_kernel(place_ref, height_ref, w_ref, sy_ref, *refs):
    u_refs, g_ref = refs[:STA], refs[STA]
    first = (slab_pos() * XL).astype(jnp.float32)
    yy = iota((1, NY), 1).astype(jnp.float32) + 0.5
    rows = 16

    for s in range(STA):
        east0 = place_ref[0:1, s : s + 1] * float(NX)
        north2 = (yy - place_ref[1:2, s : s + 1] * float(NY)) ** 2
        height = height_ref[0:1, s : s + 1]

        def body(i, _):
            z0 = pl.multiple_of(i * rows, rows)
            zz = (z0 + iota((rows, 1), 0)).astype(jnp.float32) + 0.5 + height
            base = north2 + zz * zz
            lead = jnp.broadcast_to(SCALE * zz, (rows, NY))

            def leaf(x):
                east = (first + (x + 0.5)) - east0
                r = lax.rsqrt(base + east * east)
                return (w_ref[x, pl.ds(z0, rows), :] * lead) * (r * r * r)

            def put(tab, value):
                at = pl.ds(pl.multiple_of((s * XL + tab) * NZ + z0, rows), rows)
                high, low = split(value, 2)
                g_ref[at, 0:NY] = high
                g_ref[at, NY : 2 * NY] = low

            def tree(x, width):
                if width == 1:
                    return leaf(x)
                left = tree(x, width // 2)
                right = tree(x + width // 2, width // 2)
                start = {2: 0, 4: 8, 8: 12, 16: 14}[width]
                put(start + x // width, left - right)
                return left + right

            put(XL - 1, tree(0, XL))
            return 0

        lax.fori_loop(0, NZ // rows, body, 0)

    for i in range(TABS * NZ // 256):
        s, at = divmod(i * 256, XL * NZ)
        u_refs[s][:, at : at + 256] = lax.dot_general(
            sy_ref[...],
            g_ref[i * 256 : (i + 1) * 256, :],
            (((1,), (1,)), ((), ())),
            preferred_element_type=jnp.float32,
        )


def message_kernel(code_ref, *refs):
    u_refs, out_ref = refs[:STA], refs[STA]
    half_y = NY // 2
    low_half = iota((8, 128), 1) < NZ
    column_id = iota((FINE, 256), 1)

    def body(j, _):
        at = pl.multiple_of(j * HALF, HALF)
        at1 = pl.multiple_of(half_y + j * HALF, HALF)
        for s in range(STA):
            lanes = slice((XL - 2) * NZ, XL * NZ)
            u0 = u_refs[s][pl.ds(at, HALF), lanes]
            u1 = u_refs[s][pl.ds(at1, HALF), lanes]
            out_ref[j, s * HALF : (s + 1) * HALF, :] = jnp.where(low_half, pltpu.roll(u0, NZ, 1), u1)
        both = []
        for t in (at, at1):
            both.append(
                jnp.concatenate(
                    [u[pl.ds(t, HALF), q * 128 : (q + 1) * 128] for u in u_refs for q in range(XL // 2)], axis=0
                )
            )
        table = jnp.concatenate(both, axis=1)
        high, low = split(table, 2)
        code = code_ref[j]
        wide = jnp.concatenate([code, code], axis=1)
        known = jnp.where(wide >= 0, wide & 255, -1)
        pick = jnp.where(known == column_id, 1.0, 0.0).astype(jnp.bfloat16)
        got = jnp.dot(pick, high, preferred_element_type=jnp.float32)
        got = got + jnp.dot(pick, low, preferred_element_type=jnp.float32)
        v0, v1 = got[:, :128], got[:, 128:]
        even = jnp.where(low_half, v0, pltpu.roll(v1, NZ, 1))
        odd = jnp.where(low_half, pltpu.roll(v0, NZ, 1), v1)
        out_ref[j, COARSE:MSG, :] = jnp.where(code >= 256, odd, even)
        return 0

    lax.fori_loop(0, SLABS, body, 0, unroll=2)


def power(level_top, value):
    out = jnp.full(value.shape, 2.0 ** (-level_top / 2), jnp.float32)
    for level in range(1, level_top):
        out = jnp.where(value >= (1 << level), np.float32(2.0 ** (-(level_top - level) / 2)), out)
    return out


def index_kernel(kept_ref, dest_ref, sx_ref, coarse_ref, fine_ref, spot_ref, scale_ref):
    k = column(kept_ref[...].astype(jnp.float32)).astype(jnp.int32)
    a, pair, xs, _ = places_of(k)
    rank = earlier(xs.astype(jnp.float32)).astype(jnp.int32)
    one_a = jnp.where(iota((ROWS, SLABS), 1) == a, 1.0, 0.0).astype(jnp.bfloat16)
    sign = jnp.dot(one_a, sx_ref[...], preferred_element_type=jnp.float32)
    mine = station_col() * HALF + pair
    there = (iota((ROWS, SLABS * COARSE), 1) & (COARSE - 1)) == mine
    coarse_ref[...] = jnp.where(there, sign, 0.0).astype(jnp.bfloat16)
    key = jnp.where(xs < SLABS, xs * FINE + rank, -1)
    fine_ref[...] = jnp.where(iota((ROWS, SLABS * FINE), 1) == key, 1.0, 0.0).astype(jnp.bfloat16)
    dest = column(dest_ref[...].astype(jnp.float32))
    spot = turned(dest * 8.0 + earlier(dest)).astype(jnp.int32)
    where = jnp.broadcast_to(spot, (OWNERS * 8, ROWS)) == iota((OWNERS * 8, ROWS), 0)
    spot_ref[...] = jnp.where(where, 1.0, 0.0).astype(jnp.bfloat16)
    b = 2 * (slab_pos() * HALF + pair)
    rowscale = power(8, a) * power(8, b)
    lanescale = power(6, iota((ROWS, LANES), 1) & (NZ - 1))
    scale_ref[...] = rowscale * lanescale


def dots(pick, parts):
    total = jnp.dot(pick, parts[0], preferred_element_type=jnp.float32)
    for part in parts[1:]:
        total = total + jnp.dot(pick, part, preferred_element_type=jnp.float32)
    return total


def combine_kernel(got_ref, coarse_ref, fine_ref, spot_ref, scale_ref, sz_ref, out_ref):
    coarse = got_ref[:, 0:COARSE, :].reshape(SLABS * COARSE, LANES)
    fine = got_ref[:, COARSE:MSG, :].reshape(SLABS * FINE, LANES)
    value = dots(coarse_ref[...], split(coarse, 3)) + dots(fine_ref[...], split(fine, 3))
    value = jnp.dot(jnp.concatenate(split(value, 3), axis=1), sz_ref[...], preferred_element_type=jnp.float32)
    value = value * scale_ref[...]
    placed = dots(spot_ref[...], split(value, 3))
    out_ref[...] = placed.reshape(OWNERS, 8, LANES)


def call(body, outs, scratch=(), cost=None, limit=16):
    vmem = pl.BlockSpec(memory_space=pltpu.VMEM)
    many = isinstance(outs, (list, tuple))
    return functools.partial(
        pl.pallas_call,
        body,
        out_shape=outs,
        out_specs=[vmem] * len(outs) if many else vmem,
        scratch_shapes=list(scratch),
        compiler_params=pltpu.CompilerParams(vmem_limit_bytes=limit * MIB),
        cost_estimate=cost,
    )


def run(make, *args):
    vmem = pl.BlockSpec(memory_space=pltpu.VMEM)
    return make(in_specs=[vmem] * len(args))(*args)


def struct(shape, dtype=jnp.float32):
    return jax.ShapeDtypeStruct(shape, dtype)


def lists(kept):
    return run(call(list_kernel, struct((SLABS, FINE, 128), jnp.int32)), kept)


def tables(place, height, weight, sy):
    cost = pl.CostEstimate(flops=2 * 512 * 256 * 4096, bytes_accessed=6 * MIB, transcendentals=1 << 20)
    return run(
        call(
            table_kernel,
            [struct((NY, XL * NZ))] * STA,
            [pltpu.VMEM((TABS * NZ, 2 * NY), jnp.bfloat16)],
            cost,
        ),
        place.T,
        height.reshape(1, STA),
        jnp.transpose(weight, (0, 2, 1)),
        sy,
    )


def messages(codes, u):
    return run(call(message_kernel, struct((SLABS, MSG, LANES))), codes, *u)


def indices(kept, dest, sx):
    bf = jnp.bfloat16
    outs = [
        struct((ROWS, SLABS * COARSE), bf),
        struct((ROWS, SLABS * FINE), bf),
        struct((OWNERS * 8, ROWS), bf),
        struct((ROWS, LANES)),
    ]
    return run(call(index_kernel, outs), kept, dest, sx)


def combined(got, index, sz):
    return run(call(combine_kernel, struct((OWNERS, 8, LANES))), got, *index, sz)


def local(station_place, station_height, cell_weight, kept, dest):
    sy, sz, sx = (jnp.asarray(c) for c in constants())
    kept = kept.reshape(STA, KEEP)
    dest = dest.reshape(STA, KEEP)
    codes = lax.all_to_all(lists(kept), "slab", 0, 0, tiled=True)
    u = tables(station_place, station_height, cell_weight, sy)
    got = lax.all_to_all(messages(codes, u), "slab", 0, 0, tiled=True)
    index = indices(kept, dest, sx)
    out = lax.all_to_all(combined(got, index, sz), "sta", 0, 0, tiled=True)
    return out[None, None, :, :CAP, :]


def solution(mesh):
    placed = (
        P("sta", None),
        P("sta"),
        P("slab", None, None),
        P("slab", "sta", None),
        P("slab", "sta", None, None),
    )
    return jax.shard_map(
        local,
        mesh=mesh,
        in_specs=placed,
        out_specs=P("slab", "sta", None, None, None),
        check_vma=False,
    )
```

```python
import jax
import jax.numpy as jnp
import numpy as np
from jax import lax
from jax.experimental import pallas as pl
from jax.experimental.pallas import tpu as pltpu
from jax.sharding import PartitionSpec as P

SCALE = 32.0
SLABS = 16
OWNERS = 32
STA = 4
KEEP = 16
ROWS = STA * KEEP
XL = 16
NX = 256
NY = 256
NZ = 64
HALF = 8
CAP = 6
FINE = 8
COARSE = STA * HALF
MSG = COARSE + FINE
LANES = 2 * NZ
TABS = STA * XL
MIB = 1 << 20
GRANT = 52000 << 10
FAR = 30


def signs(order):
    out = np.zeros((order, order), np.float32)
    out[0] = 1
    count = 1
    while count < order:
        width = order // count
        for k in range(count):
            out[count + k, k * width : k * width + width // 2] = 1
            out[count + k, k * width + width // 2 : (k + 1) * width] = -1
        count *= 2
    return out


def constants():
    sy = signs(NY)
    sy = np.concatenate([sy[0::2], sy[1::2]], axis=0)
    sz = np.zeros((LANES, LANES), np.float32)
    sz[:NZ, :NZ] = signs(NZ).T
    sz[NZ:, NZ:] = signs(NZ).T
    sz = np.concatenate([sz] * 3, axis=0)
    sx = np.repeat(signs(SLABS), COARSE, axis=1)
    bf = jnp.bfloat16
    return np.asarray(sy, bf), np.asarray(sz, bf), np.asarray(sx, bf)


def slab_pos():
    return lax.axis_index("slab")


def iota(shape, dim):
    return lax.broadcasted_iota(jnp.int32, shape, dim)


def column(tile):
    eye = iota((KEEP, KEEP), 0) == iota((KEEP, KEEP), 1)
    parts = []
    for s in range(STA):
        row = jnp.broadcast_to(tile[s : s + 1, :], (KEEP, KEEP))
        parts.append(jnp.sum(jnp.where(eye, row, 0.0), axis=1, keepdims=True))
    return jnp.concatenate(parts, axis=0)


def turned(col):
    eye = iota((ROWS, ROWS), 0) == iota((ROWS, ROWS), 1)
    wide = jnp.broadcast_to(col, (ROWS, ROWS))
    return jnp.sum(jnp.where(eye, wide, 0.0), axis=0, keepdims=True)


def earlier(col):
    row = turned(col)
    before = iota((ROWS, ROWS), 1) < iota((ROWS, ROWS), 0)
    same = (jnp.broadcast_to(row, (ROWS, ROWS)) == jnp.broadcast_to(col, (ROWS, ROWS))) & before
    return jnp.sum(jnp.where(same, 1.0, 0.0), axis=1, keepdims=True)


def split(x, parts):
    out = []
    for i in range(parts):
        piece = x.astype(jnp.bfloat16)
        out.append(piece)
        if i + 1 < parts:
            x = x - piece.astype(jnp.float32)
    return out


def places_of(k):
    a = lax.shift_right_logical(k, 3)
    pair = k & (HALF - 1)
    xs = jnp.full_like(a, SLABS)
    tab = jnp.full_like(a, XL - 1)
    for least, shift, base in ((16, 0, 14), (32, 1, 12), (64, 2, 8), (128, 3, 0)):
        inside = a >= least
        off = a - least
        xs = jnp.where(inside, lax.shift_right_logical(off, shift), xs)
        tab = jnp.where(inside, base + (off & ((1 << shift) - 1)), tab)
    return a, pair, xs, tab


def station_col():
    return lax.shift_right_logical(iota((ROWS, 1), 0), 4)


def list_kernel(kept_ref, place_ref, height_ref, sy_ref, out_ref, place_out, height_out, sy_out):
    sy_out[...] = sy_ref[...]
    place_out[...] = place_ref[...]
    height_out[...] = height_ref[...]
    k = column(kept_ref[...].astype(jnp.float32)).astype(jnp.int32)
    _, pair, xs, tab = places_of(k)
    table = station_col() * XL + tab
    row = (slab_pos() & 1) * HALF + pair
    code = (table & 1) * (16 * TABS // 2) + lax.shift_right_logical(table, 1) * 16 + row
    rank = earlier(xs.astype(jnp.float32)).astype(jnp.int32)
    key = turned((xs * FINE + rank).astype(jnp.float32)).astype(jnp.int32)
    coderow = turned(code.astype(jnp.float32))
    count = SLABS * FINE
    hit = jnp.broadcast_to(key, (count, ROWS)) == iota((count, ROWS), 0)
    found = jnp.sum(jnp.where(hit, jnp.broadcast_to(coderow, (count, ROWS)) + 1.0, 0.0), axis=1, keepdims=True)
    tile = jnp.broadcast_to(found - 1.0, (count, 128)).astype(jnp.int32)
    out_ref[...] = tile.reshape(SLABS, FINE, 128)


PART = XL * NZ


def table_kernel(place_ref, height_ref, w_hbm, sy_ref, far_ref, *refs):
    outs = refs[: STA - 1]
    w_ref, g_ref, own_ref, w_sems, sem = refs[STA - 1 :]
    first = (slab_pos() * XL).astype(jnp.float32)
    yy = iota((1, NY), 1).astype(jnp.float32) + 0.5
    rows = 16
    arrivals = []
    for i in range(NZ // rows):
        at = (slice(None), pl.ds(i * rows, rows))
        arrivals.append(pltpu.make_async_copy(w_hbm.at[at], w_ref.at[at], w_sems.at[i]))
        arrivals[-1].start()

    def field(s):
        east0 = place_ref[0:1, s : s + 1] * float(NX)
        north2 = (yy - place_ref[1:2, s : s + 1] * float(NY)) ** 2
        height = height_ref[0:1, s : s + 1]
        for z0 in range(0, NZ, rows):
            if s == 0:
                arrivals[z0 // rows].wait()
            zz = (z0 + iota((rows, 1), 0)).astype(jnp.float32) + 0.5 + height
            base = north2 + zz * zz
            lead = jnp.broadcast_to(SCALE * zz, (rows, NY))

            def leaf(x):
                east = (first + (x + 0.5)) - east0
                r = lax.rsqrt(base + east * east)
                return (w_ref[x, z0 : z0 + rows, :] * lead) * (r * r * r)

            def put(tab, value):
                at = slice((s * XL + tab) * NZ + z0, (s * XL + tab) * NZ + z0 + rows)
                high, low = split(value, 2)
                g_ref[at, 0:NY] = high
                g_ref[at, NY : 2 * NY] = low

            def tree(x, width):
                if width == 1:
                    return leaf(x)
                left = tree(x, width // 2)
                right = tree(x + width // 2, width // 2)
                start = {2: 0, 4: 8, 8: 12, 16: 14}[width]
                put(start + x // width, left - right)
                return left + right

            put(XL - 1, tree(0, XL))

    def product(s):
        to = outs[s - 1] if s else own_ref
        for i in range(PART // 256):
            g = g_ref[s * PART + i * 256 : s * PART + (i + 1) * 256, :]
            u = lax.dot_general(
                jnp.concatenate([sy_ref[...]] * 2, axis=1),
                g,
                (((1,), (1,)), ((), ())),
                preferred_element_type=jnp.float32,
            )
            high, low = split(u, 2)
            to[:, i * 256 : (i + 1) * 256] = high
            to[:, PART + i * 256 : PART + (i + 1) * 256] = low

    copy = pltpu.make_async_copy(own_ref, far_ref.at[0], sem)
    for s in range(STA):
        field(s)
        if s:
            product(s - 1)
        if s == 1:
            copy.start()
    product(STA - 1)
    copy.wait()


def message_kernel(code_ref, far_ref, *refs):
    u_refs, out_ref, near_ref, sem = refs[: STA - 1], refs[STA - 1], refs[STA], refs[STA + 1]
    copy = pltpu.make_async_copy(far_ref.at[0], near_ref, sem)
    copy.start()
    low_half = iota((16, 128), 1) < NZ
    column_id = iota((16, 256), 1)
    groups = SLABS // 2

    def rows_of(g, t):
        return slice(t * (NY // 2) + g * 16, t * (NY // 2) + g * 16 + 16)

    def known(g):
        code = code_ref[2 * g : 2 * g + 2].reshape(16, 128)
        wide = jnp.concatenate([code, code], axis=1)
        return code, jnp.where(wide >= 0, wide & 511, -1)

    def picked(g, tables, base):
        pick = jnp.where(known(g)[1] == column_id + base, 1.0, 0.0).astype(jnp.bfloat16)
        total = None
        for part in (0, PART):
            both = []
            for t in (0, 1):
                both.append(
                    jnp.concatenate(
                        [u[rows_of(g, t), part + q * 128 : part + (q + 1) * 128] for u in tables for q in range(XL // 2)],
                        axis=0,
                    )
                )
            got = jnp.dot(pick, jnp.concatenate(both, axis=1), preferred_element_type=jnp.float32)
            total = got if total is None else total + got
        return total

    def coarse(g, s, u):
        lanes = PART - 128
        v = []
        for t in (0, 1):
            high = u[rows_of(g, t), lanes : lanes + 128].astype(jnp.float32)
            v.append(high + u[rows_of(g, t), PART + lanes : PART + lanes + 128].astype(jnp.float32))
        row = jnp.where(low_half, pltpu.roll(v[0], NZ, 1), v[1])
        out_ref[2 * g : 2 * g + 2, s * HALF : (s + 1) * HALF, :] = row.reshape(2, HALF, 128)

    got = [picked(g, u_refs[1:], 256) for g in range(groups)]
    for g in range(groups):
        for s in range(1, STA):
            coarse(g, s, u_refs[s - 1])
    copy.wait()
    for g in range(groups):
        coarse(g, 0, near_ref)
        both = got[g] + picked(g, (near_ref, u_refs[0]), 0)
        v0, v1 = both[:, :128], both[:, 128:]
        even = jnp.where(low_half, v0, pltpu.roll(v1, NZ, 1))
        odd = jnp.where(low_half, pltpu.roll(v0, NZ, 1), v1)
        fine = jnp.where(known(g)[0] >= 512, odd, even)
        out_ref[2 * g : 2 * g + 2, COARSE:MSG, :] = fine.reshape(2, FINE, 128)


def power(level_top, value):
    out = jnp.full(value.shape, 2.0 ** (-level_top / 2), jnp.float32)
    for level in range(1, level_top):
        out = jnp.where(value >= (1 << level), np.float32(2.0 ** (-(level_top - level) / 2)), out)
    return out


def index_kernel(kept_ref, dest_ref, sx_ref, coarse_ref, fine_ref, spot_ref, scale_ref):
    k = column(kept_ref[...].astype(jnp.float32)).astype(jnp.int32)
    a, pair, xs, _ = places_of(k)
    rank = earlier(xs.astype(jnp.float32)).astype(jnp.int32)
    one_a = jnp.where(iota((ROWS, SLABS), 1) == a, 1.0, 0.0).astype(jnp.bfloat16)
    sign = jnp.dot(one_a, sx_ref[...], preferred_element_type=jnp.float32)
    mine = station_col() * HALF + pair
    there = (iota((ROWS, SLABS * COARSE), 1) & (COARSE - 1)) == mine
    coarse_ref[...] = jnp.where(there, sign, 0.0).astype(jnp.bfloat16)
    key = jnp.where(xs < SLABS, xs * FINE + rank, -1)
    fine_ref[...] = jnp.where(iota((ROWS, SLABS * FINE), 1) == key, 1.0, 0.0).astype(jnp.bfloat16)
    dest = column(dest_ref[...].astype(jnp.float32))
    spot = turned(dest * 8.0 + earlier(dest)).astype(jnp.int32)
    where = jnp.broadcast_to(spot, (OWNERS * 8, ROWS)) == iota((OWNERS * 8, ROWS), 0)
    spot_ref[...] = jnp.where(where, 1.0, 0.0).astype(jnp.bfloat16)
    b = 2 * (slab_pos() * HALF + pair)
    rowscale = power(8, a) * power(8, b)
    lanescale = power(6, iota((ROWS, LANES), 1) & (NZ - 1))
    scale_ref[...] = rowscale * lanescale


def dots(pick, parts):
    total = jnp.dot(pick, parts[0], preferred_element_type=jnp.float32)
    for part in parts[1:]:
        total = total + jnp.dot(pick, part, preferred_element_type=jnp.float32)
    return total


def combine_kernel(got_ref, coarse_ref, fine_ref, spot_ref, scale_ref, sz_ref, out_ref):
    coarse = got_ref[:, 0:COARSE, :].reshape(SLABS * COARSE, LANES)
    fine = got_ref[:, COARSE:MSG, :].reshape(SLABS * FINE, LANES)
    value = dots(coarse_ref[...], split(coarse, 3)) + dots(fine_ref[...], split(fine, 3))
    value = jnp.dot(jnp.concatenate(split(value, 3), axis=1), sz_ref[...], preferred_element_type=jnp.float32)
    value = value * scale_ref[...]
    placed = dots(spot_ref[...], split(value, 3))
    out_ref[...] = placed.reshape(OWNERS, 8, LANES)


VMEM = pl.BlockSpec(memory_space=pltpu.VMEM)
HBM = pl.BlockSpec(memory_space=pltpu.HBM)


def run(body, args, ins, shapes, outs, scratch=(), cost=None, limit=16 * MIB):
    return pl.pallas_call(
        body,
        out_shape=shapes,
        in_specs=ins,
        out_specs=outs,
        scratch_shapes=list(scratch),
        compiler_params=pltpu.CompilerParams(vmem_limit_bytes=limit),
        cost_estimate=cost,
    )(*args)


def struct(shape, dtype=jnp.float32):
    return jax.ShapeDtypeStruct(shape, dtype)


def lists(kept, place, height, sy):
    return run(
        list_kernel,
        (kept, place.T, height.reshape(1, STA), sy),
        [VMEM] * 4,
        [
            struct((SLABS, FINE, 128), jnp.int32),
            struct((2, STA)),
            struct((1, STA)),
            struct((NY, NY), jnp.bfloat16),
        ],
        [VMEM] * 4,
    )


def tables(place, height, weight, sy):
    cost = pl.CostEstimate(flops=2 * 512 * 256 * 4096, bytes_accessed=6 * MIB, transcendentals=1 << 20)
    part = struct((NY, 2 * PART), jnp.bfloat16)
    return run(
        table_kernel,
        (place, height, jnp.transpose(weight, (0, 2, 1)), sy),
        [VMEM, VMEM, HBM, VMEM],
        [struct((FAR, NY, 2 * PART), jnp.bfloat16)] + [part] * (STA - 1),
        [HBM] + [VMEM] * (STA - 1),
        [
            pltpu.VMEM((XL, NZ, NY), jnp.float32),
            pltpu.VMEM((TABS * NZ, 2 * NY), jnp.bfloat16),
            pltpu.VMEM((NY, 2 * PART), jnp.bfloat16),
            pltpu.SemaphoreType.DMA((NZ // 16,)),
            pltpu.SemaphoreType.DMA,
        ],
        cost,
        GRANT,
    )


def messages(codes, u):
    return run(
        message_kernel,
        (codes, *u),
        [VMEM, HBM] + [VMEM] * (STA - 1),
        struct((SLABS, MSG, LANES)),
        VMEM,
        [pltpu.VMEM((NY, 2 * PART), jnp.bfloat16), pltpu.SemaphoreType.DMA],
        None,
        44 * MIB,
    )


def indices(kept, dest, sx):
    bf = jnp.bfloat16
    outs = [
        struct((ROWS, SLABS * COARSE), bf),
        struct((ROWS, SLABS * FINE), bf),
        struct((OWNERS * 8, ROWS), bf),
        struct((ROWS, LANES)),
    ]
    return run(index_kernel, (kept, dest, sx), [VMEM] * 3, outs, [VMEM] * 4)


def combined(got, index, sz):
    return run(combine_kernel, (got, *index, sz), [VMEM] * 6, struct((OWNERS, 8, LANES)), VMEM)


def local(station_place, station_height, cell_weight, kept, dest):
    sy, sz, sx = (jnp.asarray(c) for c in constants())
    kept = kept.reshape(STA, KEEP)
    dest = dest.reshape(STA, KEEP)
    codes, place, height, sy = lists(kept, station_place, station_height, sy)
    codes = lax.all_to_all(codes, "slab", 0, 0, tiled=True)
    u = tables(place, height, cell_weight, sy)
    got = lax.all_to_all(messages(codes, u), "slab", 0, 0, tiled=True)
    index = indices(kept, dest, sx)
    out = lax.all_to_all(combined(got, index, sz), "sta", 0, 0, tiled=True)
    return out[None, None, :, :CAP, :]


def solution(mesh):
    placed = (
        P("sta", None),
        P("sta"),
        P("slab", None, None),
        P("slab", "sta", None),
        P("slab", "sta", None, None),
    )
    return jax.shard_map(
        local,
        mesh=mesh,
        in_specs=placed,
        out_specs=P("slab", "sta", None, None, None),
        check_vma=False,
    )
```

```python
import jax
import jax.numpy as jnp
import numpy as np
from jax import lax
from jax.experimental import pallas as pl
from jax.experimental.pallas import tpu as pltpu
from jax.sharding import PartitionSpec as P

SCALE = 32.0
SLABS = 16
OWNERS = 32
STA = 4
KEEP = 16
ROWS = STA * KEEP
XL = 16
NX = 256
NY = 256
NZ = 64
HALF = 8
CAP = 6
FINE = 8
COARSE = STA * HALF
MSG = COARSE + FINE
LANES = 2 * NZ
TABS = STA * XL
MIB = 1 << 20
GRANT = 52000 << 10
FAR = 30


def signs(order):
    out = np.zeros((order, order), np.float32)
    out[0] = 1
    count = 1
    while count < order:
        width = order // count
        for k in range(count):
            out[count + k, k * width : k * width + width // 2] = 1
            out[count + k, k * width + width // 2 : (k + 1) * width] = -1
        count *= 2
    return out


def constants():
    sz = np.zeros((LANES, LANES), np.float32)
    sz[:NZ, :NZ] = signs(NZ).T
    sz[NZ:, NZ:] = signs(NZ).T
    sz = np.concatenate([sz] * 3, axis=0)
    sx = np.repeat(signs(SLABS), COARSE, axis=1)
    bf = jnp.bfloat16
    return np.asarray(sz, bf), np.asarray(sx, bf)


def slab_pos():
    return lax.axis_index("slab")


def iota(shape, dim):
    return lax.broadcasted_iota(jnp.int32, shape, dim)


def column(tile):
    eye = iota((KEEP, KEEP), 0) == iota((KEEP, KEEP), 1)
    parts = []
    for s in range(STA):
        row = jnp.broadcast_to(tile[s : s + 1, :], (KEEP, KEEP))
        parts.append(jnp.sum(jnp.where(eye, row, 0.0), axis=1, keepdims=True))
    return jnp.concatenate(parts, axis=0)


def turned(col):
    eye = iota((ROWS, ROWS), 0) == iota((ROWS, ROWS), 1)
    wide = jnp.broadcast_to(col, (ROWS, ROWS))
    return jnp.sum(jnp.where(eye, wide, 0.0), axis=0, keepdims=True)


def earlier(col):
    row = turned(col)
    before = iota((ROWS, ROWS), 1) < iota((ROWS, ROWS), 0)
    same = (jnp.broadcast_to(row, (ROWS, ROWS)) == jnp.broadcast_to(col, (ROWS, ROWS))) & before
    return jnp.sum(jnp.where(same, 1.0, 0.0), axis=1, keepdims=True)


def split(x, parts):
    out = []
    for i in range(parts):
        piece = x.astype(jnp.bfloat16)
        out.append(piece)
        if i + 1 < parts:
            x = x - piece.astype(jnp.float32)
    return out


def places_of(k):
    a = lax.shift_right_logical(k, 3)
    pair = k & (HALF - 1)
    xs = jnp.full_like(a, SLABS)
    tab = jnp.full_like(a, XL - 1)
    for least, shift, base in ((16, 0, 14), (32, 1, 12), (64, 2, 8), (128, 3, 0)):
        inside = a >= least
        off = a - least
        xs = jnp.where(inside, lax.shift_right_logical(off, shift), xs)
        tab = jnp.where(inside, base + (off & ((1 << shift) - 1)), tab)
    return a, pair, xs, tab


def station_col():
    return lax.shift_right_logical(iota((ROWS, 1), 0), 4)


def list_kernel(kept_ref, out_ref):
    k = column(kept_ref[...].astype(jnp.float32)).astype(jnp.int32)
    _, pair, xs, tab = places_of(k)
    table = station_col() * XL + tab
    row = (slab_pos() & 1) * HALF + pair
    code = (table & 1) * (16 * TABS // 2) + lax.shift_right_logical(table, 1) * 16 + row
    rank = earlier(xs.astype(jnp.float32)).astype(jnp.int32)
    key = turned((xs * FINE + rank).astype(jnp.float32)).astype(jnp.int32)
    coderow = turned(code.astype(jnp.float32))
    count = SLABS * FINE
    hit = jnp.broadcast_to(key, (count, ROWS)) == iota((count, ROWS), 0)
    found = jnp.sum(jnp.where(hit, jnp.broadcast_to(coderow, (count, ROWS)) + 1.0, 0.0), axis=1, keepdims=True)
    tile = jnp.broadcast_to(found - 1.0, (count, 128)).astype(jnp.int32)
    out_ref[...] = tile.reshape(SLABS, FINE, 128)


PART = XL * NZ


def haar_signs():
    row = iota((NY, 1), 0)
    b = 2 * (row & (NY // 2 - 1)) + lax.shift_right_logical(row, 7)
    start = jnp.zeros_like(b)
    width = jnp.full_like(b, NY)
    for level in range(1, 8):
        inside = b >= (1 << level)
        width = jnp.where(inside, NY >> level, width)
        start = jnp.where(inside, (b - (1 << level)) * (NY >> level), start)
    middle = jnp.where(b == 0, start + width, start + lax.shift_right_logical(width, 1))
    y = iota((NY, NY), 1)
    signed = jnp.where(y < middle, 1.0, jnp.where(y < start + width, -1.0, 0.0))
    signed = jnp.where(y < start, 0.0, signed).astype(jnp.bfloat16)
    return jnp.concatenate([signed, signed], axis=1)


def table_kernel(place_ref, height_ref, w_hbm, far_ref, *refs):
    outs = refs[: STA - 1]
    w_ref, sy_ref, g_ref, own_ref, w_sems, sem = refs[STA - 1 :]
    first = (slab_pos() * XL).astype(jnp.float32)
    yy = iota((1, NY), 1).astype(jnp.float32) + 0.5
    rows = 16
    arrivals = []
    for i in range(NZ // rows):
        at = (slice(None), pl.ds(i * rows, rows))
        arrivals.append(pltpu.make_async_copy(w_hbm.at[at], w_ref.at[at], w_sems.at[i]))
        arrivals[-1].start()
    sy_ref[...] = haar_signs()

    def field(s):
        east0 = place_ref[0:1, s : s + 1] * float(NX)
        north2 = (yy - place_ref[1:2, s : s + 1] * float(NY)) ** 2
        height = height_ref[0:1, s : s + 1]
        for z0 in range(0, NZ, rows):
            if s == 0:
                arrivals[z0 // rows].wait()
            zz = (z0 + iota((rows, 1), 0)).astype(jnp.float32) + 0.5 + height
            base = north2 + zz * zz
            lead = jnp.broadcast_to(SCALE * zz, (rows, NY))

            def leaf(x):
                east = (first + (x + 0.5)) - east0
                r = lax.rsqrt(base + east * east)
                return (w_ref[x, z0 : z0 + rows, :] * lead) * (r * r * r)

            def put(tab, value):
                at = slice((s * XL + tab) * NZ + z0, (s * XL + tab) * NZ + z0 + rows)
                high, low = split(value, 2)
                g_ref[at, 0:NY] = high
                g_ref[at, NY : 2 * NY] = low

            def tree(x, width):
                if width == 1:
                    return leaf(x)
                left = tree(x, width // 2)
                right = tree(x + width // 2, width // 2)
                start = {2: 0, 4: 8, 8: 12, 16: 14}[width]
                put(start + x // width, left - right)
                return left + right

            put(XL - 1, tree(0, XL))

    def product(s):
        to = outs[s - 1] if s else own_ref
        for i in range(PART // 256):
            g = g_ref[s * PART + i * 256 : s * PART + (i + 1) * 256, :]
            u = lax.dot_general(
                sy_ref[...],
                g,
                (((1,), (1,)), ((), ())),
                preferred_element_type=jnp.float32,
            )
            high, low = split(u, 2)
            to[:, i * 256 : (i + 1) * 256] = high
            to[:, PART + i * 256 : PART + (i + 1) * 256] = low

    copy = pltpu.make_async_copy(own_ref, far_ref.at[0], sem)
    for s in range(STA):
        field(s)
        if s:
            product(s - 1)
        if s == 1:
            copy.start()
    product(STA - 1)
    copy.wait()


def message_kernel(code_ref, far_ref, *refs):
    u_refs = refs[: STA - 1]
    out_hbm, out_ref, near_ref, sems, sem = refs[STA - 1 :]
    copy = pltpu.make_async_copy(far_ref.at[0], near_ref, sem)
    copy.start()
    low_half = iota((16, 128), 1) < NZ
    column_id = iota((16, 256), 1)
    groups = SLABS // 2

    def rows_of(g, t):
        return slice(t * (NY // 2) + g * 16, t * (NY // 2) + g * 16 + 16)

    def known(g):
        code = code_ref[2 * g : 2 * g + 2].reshape(16, 128)
        wide = jnp.concatenate([code, code], axis=1)
        return code, jnp.where(wide >= 0, wide & 511, -1)

    def picked(g, tables, base):
        pick = jnp.where(known(g)[1] == column_id + base, 1.0, 0.0).astype(jnp.bfloat16)
        total = None
        for part in (0, PART):
            both = []
            for t in (0, 1):
                both.append(
                    jnp.concatenate(
                        [u[rows_of(g, t), part + q * 128 : part + (q + 1) * 128] for u in tables for q in range(XL // 2)],
                        axis=0,
                    )
                )
            got = jnp.dot(pick, jnp.concatenate(both, axis=1), preferred_element_type=jnp.float32)
            total = got if total is None else total + got
        return total

    def coarse(g, s, u):
        lanes = PART - 128
        v = []
        for t in (0, 1):
            high = u[rows_of(g, t), lanes : lanes + 128].astype(jnp.float32)
            v.append(high + u[rows_of(g, t), PART + lanes : PART + lanes + 128].astype(jnp.float32))
        row = jnp.where(low_half, pltpu.roll(v[0], NZ, 1), v[1])
        out_ref[2 * g : 2 * g + 2, s * HALF : (s + 1) * HALF, :] = row.reshape(2, HALF, 128)

    got = [picked(g, u_refs[1:], 256) for g in range(groups)]
    for g in range(groups):
        for s in range(1, STA):
            coarse(g, s, u_refs[s - 1])
    copy.wait()
    leaving = []
    for g in range(groups):
        coarse(g, 0, near_ref)
        both = got[g] + picked(g, (near_ref, u_refs[0]), 0)
        v0, v1 = both[:, :128], both[:, 128:]
        even = jnp.where(low_half, v0, pltpu.roll(v1, NZ, 1))
        odd = jnp.where(low_half, pltpu.roll(v0, NZ, 1), v1)
        fine = jnp.where(known(g)[0] >= 512, odd, even)
        out_ref[2 * g : 2 * g + 2, COARSE:MSG, :] = fine.reshape(2, FINE, 128)
        at = pl.ds(2 * g, 2)
        leaving.append(pltpu.make_async_copy(out_ref.at[at], out_hbm.at[at], sems.at[g]))
        leaving[-1].start()
    for gone in leaving:
        gone.wait()


def power(level_top, value):
    out = jnp.full(value.shape, 2.0 ** (-level_top / 2), jnp.float32)
    for level in range(1, level_top):
        out = jnp.where(value >= (1 << level), np.float32(2.0 ** (-(level_top - level) / 2)), out)
    return out


def index_kernel(kept_ref, dest_ref, sx_ref, coarse_ref, fine_ref, spot_ref, scale_ref):
    k = column(kept_ref[...].astype(jnp.float32)).astype(jnp.int32)
    a, pair, xs, _ = places_of(k)
    rank = earlier(xs.astype(jnp.float32)).astype(jnp.int32)
    one_a = jnp.where(iota((ROWS, SLABS), 1) == a, 1.0, 0.0).astype(jnp.bfloat16)
    sign = jnp.dot(one_a, sx_ref[...], preferred_element_type=jnp.float32)
    mine = station_col() * HALF + pair
    there = (iota((ROWS, SLABS * COARSE), 1) & (COARSE - 1)) == mine
    coarse_ref[...] = jnp.where(there, sign, 0.0).astype(jnp.bfloat16)
    key = jnp.where(xs < SLABS, xs * FINE + rank, -1)
    fine_ref[...] = jnp.where(iota((ROWS, SLABS * FINE), 1) == key, 1.0, 0.0).astype(jnp.bfloat16)
    dest = column(dest_ref[...].astype(jnp.float32))
    spot = turned(earlier(dest) * float(OWNERS) + dest).astype(jnp.int32)
    where = jnp.broadcast_to(spot, (OWNERS * CAP, ROWS)) == iota((OWNERS * CAP, ROWS), 0)
    spot_ref[...] = jnp.where(where, 1.0, 0.0).astype(jnp.bfloat16)
    b = 2 * (slab_pos() * HALF + pair)
    rowscale = power(8, a) * power(8, b)
    lanescale = power(6, iota((ROWS, LANES), 1) & (NZ - 1))
    scale_ref[...] = rowscale * lanescale


def dots(pick, parts):
    total = jnp.dot(pick, parts[0], preferred_element_type=jnp.float32)
    for part in parts[1:]:
        total = total + jnp.dot(pick, part, preferred_element_type=jnp.float32)
    return total


def combine_kernel(got_ref, coarse_ref, fine_ref, spot_ref, scale_ref, sz_ref, out_ref):
    coarse = got_ref[:, 0:COARSE, :].reshape(SLABS * COARSE, LANES)
    fine = got_ref[:, COARSE:MSG, :].reshape(SLABS * FINE, LANES)
    value = dots(coarse_ref[...], split(coarse, 3)) + dots(fine_ref[...], split(fine, 3))
    value = jnp.dot(jnp.concatenate(split(value, 3), axis=1), sz_ref[...], preferred_element_type=jnp.float32)
    value = value * scale_ref[...]
    placed = dots(spot_ref[...], split(value, 3))
    for slot in range(CAP):
        rows = placed[slot * OWNERS : (slot + 1) * OWNERS]
        out_ref[:, :, slot * LANES : (slot + 1) * LANES] = rows.reshape(OWNERS, 1, LANES)


VMEM = pl.BlockSpec(memory_space=pltpu.VMEM)
HBM = pl.BlockSpec(memory_space=pltpu.HBM)


def finish_kernel(got_ref, out_ref):
    for slot in range(CAP):
        out_ref[slot] = got_ref[:, :, slot * LANES : (slot + 1) * LANES].reshape(OWNERS, LANES)


def run(body, args, ins, shapes, outs, scratch=(), cost=None, limit=16 * MIB):
    return pl.pallas_call(
        body,
        out_shape=shapes,
        in_specs=ins,
        out_specs=outs,
        scratch_shapes=list(scratch),
        compiler_params=pltpu.CompilerParams(vmem_limit_bytes=limit),
        cost_estimate=cost,
    )(*args)


def struct(shape, dtype=jnp.float32):
    return jax.ShapeDtypeStruct(shape, dtype)


def lists(kept):
    cost = pl.CostEstimate(flops=3 * 10**10, bytes_accessed=MIB, transcendentals=0)
    return run(list_kernel, (kept,), [VMEM], struct((SLABS, FINE, 128), jnp.int32), VMEM, (), cost)


def tables(place, height, weight):
    cost = pl.CostEstimate(flops=2 * 512 * 256 * 4096, bytes_accessed=6 * MIB, transcendentals=1 << 20)
    part = struct((NY, 2 * PART), jnp.bfloat16)
    return run(
        table_kernel,
        (place.T, height.reshape(1, STA), jnp.transpose(weight, (0, 2, 1))),
        [VMEM, VMEM, HBM],
        [struct((FAR, NY, 2 * PART), jnp.bfloat16)] + [part] * (STA - 1),
        [HBM] + [VMEM] * (STA - 1),
        [
            pltpu.VMEM((XL, NZ, NY), jnp.float32),
            pltpu.VMEM((NY, 2 * NY), jnp.bfloat16),
            pltpu.VMEM((TABS * NZ, 2 * NY), jnp.bfloat16),
            pltpu.VMEM((NY, 2 * PART), jnp.bfloat16),
            pltpu.SemaphoreType.DMA((NZ // 16,)),
            pltpu.SemaphoreType.DMA,
        ],
        cost,
        GRANT,
    )


def messages(codes, u):
    return run(
        message_kernel,
        (codes, *u),
        [VMEM, HBM] + [VMEM] * (STA - 1),
        struct((SLABS, MSG, LANES)),
        HBM,
        [
            pltpu.VMEM((SLABS, MSG, LANES), jnp.float32),
            pltpu.VMEM((NY, 2 * PART), jnp.bfloat16),
            pltpu.SemaphoreType.DMA((SLABS // 2,)),
            pltpu.SemaphoreType.DMA,
        ],
        None,
        44 * MIB,
    )


def indices(kept, dest, sx):
    bf = jnp.bfloat16
    outs = [
        struct((ROWS, SLABS * COARSE), bf),
        struct((ROWS, SLABS * FINE), bf),
        struct((OWNERS * CAP, ROWS), bf),
        struct((ROWS, LANES)),
    ]
    return run(index_kernel, (kept, dest, sx), [VMEM] * 3, outs, [VMEM] * 4)


def combined(got, index, sz):
    return run(combine_kernel, (got, *index, sz), [VMEM] * 6, struct((OWNERS, 1, CAP * LANES)), VMEM)


def local(station_place, station_height, cell_weight, kept, dest):
    sz, sx = (jnp.asarray(c) for c in constants())
    kept = kept.reshape(STA, KEEP)
    dest = dest.reshape(STA, KEEP)
    codes = lax.all_to_all(lists(kept), "slab", 0, 0, tiled=True)
    u = tables(station_place, station_height, cell_weight)
    got = lax.all_to_all(messages(codes, u), "slab", 0, 0, tiled=True)
    index = indices(kept, dest, sx)
    out = lax.all_to_all(combined(got, index, sz), "sta", 0, 0, tiled=True)
    out = run(finish_kernel, (out,), [VMEM], struct((CAP, OWNERS, LANES)), VMEM)
    return jnp.transpose(out, (1, 0, 2))[None, None]


def solution(mesh):
    placed = (
        P("sta", None),
        P("sta"),
        P("slab", None, None),
        P("slab", "sta", None),
        P("slab", "sta", None, None),
    )
    return jax.shard_map(
        local,
        mesh=mesh,
        in_specs=placed,
        out_specs=P("slab", "sta", None, None, None),
        check_vma=False,
    )
```

```python
import jax
import jax.numpy as jnp
import numpy as np
from jax import lax
from jax.experimental import pallas as pl
from jax.experimental.pallas import tpu as pltpu
from jax.sharding import PartitionSpec as P

SCALE = 32.0
SLABS = 16
OWNERS = 32
STA = 4
KEEP = 16
ROWS = STA * KEEP
XL = 16
NX = 256
NY = 256
NZ = 64
HALF = 8
CAP = 6
FINE = 8
COARSE = STA * HALF
MSG = COARSE + FINE
LANES = 2 * NZ
TABS = STA * XL
MIB = 1 << 20
GRANT = 52000 << 10
FAR = 30


def signs(order):
    out = np.zeros((order, order), np.float32)
    out[0] = 1
    count = 1
    while count < order:
        width = order // count
        for k in range(count):
            out[count + k, k * width : k * width + width // 2] = 1
            out[count + k, k * width + width // 2 : (k + 1) * width] = -1
        count *= 2
    return out


def constants():
    sz = np.zeros((LANES, LANES), np.float32)
    sz[:NZ, :NZ] = signs(NZ).T
    sz[NZ:, NZ:] = signs(NZ).T
    sz = np.concatenate([sz] * 3, axis=0)
    sx = np.repeat(signs(SLABS), COARSE, axis=1)
    bf = jnp.bfloat16
    return np.asarray(sz, bf), np.asarray(sx, bf)


def slab_pos():
    return lax.axis_index("slab")


def iota(shape, dim):
    return lax.broadcasted_iota(jnp.int32, shape, dim)


def column(tile):
    eye = iota((KEEP, KEEP), 0) == iota((KEEP, KEEP), 1)
    parts = []
    for s in range(STA):
        row = jnp.broadcast_to(tile[s : s + 1, :], (KEEP, KEEP))
        parts.append(jnp.sum(jnp.where(eye, row, 0.0), axis=1, keepdims=True))
    return jnp.concatenate(parts, axis=0)


def turned(col):
    eye = iota((ROWS, ROWS), 0) == iota((ROWS, ROWS), 1)
    wide = jnp.broadcast_to(col, (ROWS, ROWS))
    return jnp.sum(jnp.where(eye, wide, 0.0), axis=0, keepdims=True)


def earlier(col):
    row = turned(col)
    before = iota((ROWS, ROWS), 1) < iota((ROWS, ROWS), 0)
    same = (jnp.broadcast_to(row, (ROWS, ROWS)) == jnp.broadcast_to(col, (ROWS, ROWS))) & before
    return jnp.sum(jnp.where(same, 1.0, 0.0), axis=1, keepdims=True)


def split(x, parts):
    out = []
    for i in range(parts):
        piece = x.astype(jnp.bfloat16)
        out.append(piece)
        if i + 1 < parts:
            x = x - piece.astype(jnp.float32)
    return out


def places_of(k):
    a = lax.shift_right_logical(k, 3)
    pair = k & (HALF - 1)
    xs = jnp.full_like(a, SLABS)
    tab = jnp.full_like(a, XL - 1)
    for least, shift, base in ((16, 0, 14), (32, 1, 12), (64, 2, 8), (128, 3, 0)):
        inside = a >= least
        off = a - least
        xs = jnp.where(inside, lax.shift_right_logical(off, shift), xs)
        tab = jnp.where(inside, base + (off & ((1 << shift) - 1)), tab)
    return a, pair, xs, tab


def station_col():
    return lax.shift_right_logical(iota((ROWS, 1), 0), 4)


def list_kernel(kept_ref, out_ref):
    k = column(kept_ref[...].astype(jnp.float32)).astype(jnp.int32)
    _, pair, xs, tab = places_of(k)
    table = station_col() * XL + tab
    row = (slab_pos() & 1) * HALF + pair
    code = (table & 1) * (16 * TABS // 2) + lax.shift_right_logical(table, 1) * 16 + row
    rank = earlier(xs.astype(jnp.float32)).astype(jnp.int32)
    key = turned((xs * FINE + rank).astype(jnp.float32)).astype(jnp.int32)
    coderow = turned(code.astype(jnp.float32))
    count = SLABS * FINE
    hit = jnp.broadcast_to(key, (count, ROWS)) == iota((count, ROWS), 0)
    found = jnp.sum(jnp.where(hit, jnp.broadcast_to(coderow, (count, ROWS)) + 1.0, 0.0), axis=1, keepdims=True)
    tile = jnp.broadcast_to(found - 1.0, (count, 128)).astype(jnp.int32)
    out_ref[...] = tile.reshape(SLABS, FINE, 128)


PART = XL * NZ


def haar_signs():
    row = iota((NY, 1), 0)
    b = 2 * (row & (NY // 2 - 1)) + lax.shift_right_logical(row, 7)
    start = jnp.zeros_like(b)
    width = jnp.full_like(b, NY)
    for level in range(1, 8):
        inside = b >= (1 << level)
        width = jnp.where(inside, NY >> level, width)
        start = jnp.where(inside, (b - (1 << level)) * (NY >> level), start)
    middle = jnp.where(b == 0, start + width, start + lax.shift_right_logical(width, 1))
    y = iota((NY, NY), 1)
    signed = jnp.where(y < middle, 1.0, jnp.where(y < start + width, -1.0, 0.0))
    signed = jnp.where(y < start, 0.0, signed).astype(jnp.bfloat16)
    return jnp.concatenate([signed, signed], axis=1)


def table_kernel(place_ref, height_ref, w_hbm, far_ref, *refs):
    outs = refs[: STA - 1]
    w_ref, ready_ref, sy_ref, g_ref, own_ref, w_sems, sem = refs[STA - 1 :]
    first = (slab_pos() * XL).astype(jnp.float32)
    yy = iota((1, NY), 1).astype(jnp.float32) + 0.5
    rows = 16
    arrivals = []
    for i in range(NZ // rows):
        at = (slice(None), pl.ds(i * rows, rows))
        arrivals.append(pltpu.make_async_copy(w_hbm.at[at], w_ref.at[at], w_sems.at[i]))
        arrivals[-1].start()
    sy_ref[...] = haar_signs()

    def field(s):
        east0 = place_ref[0:1, s : s + 1] * float(NX)
        north2 = (yy - place_ref[1:2, s : s + 1] * float(NY)) ** 2
        height = height_ref[0:1, s : s + 1]

        def cells(x, z0):
            zz = (z0 + iota((rows, 1), 0)).astype(jnp.float32) + 0.5 + height
            east = (first + (x + 0.5)) - east0
            r = lax.rsqrt((north2 + zz * zz) + east * east)
            return jnp.broadcast_to(SCALE * zz, (rows, NY)) * (r * r * r)

        if s == 0:
            for z0 in range(0, NZ, rows):
                for x in range(XL):
                    ready_ref[x, z0 : z0 + rows, :] = cells(x, z0)
        for z0 in range(0, NZ, rows):
            if s == 0:
                arrivals[z0 // rows].wait()

            def leaf(x):
                known = ready_ref[x, z0 : z0 + rows, :] if s == 0 else cells(x, z0)
                return w_ref[x, z0 : z0 + rows, :] * known

            def put(tab, value):
                at = slice((s * XL + tab) * NZ + z0, (s * XL + tab) * NZ + z0 + rows)
                high, low = split(value, 2)
                g_ref[at, 0:NY] = high
                g_ref[at, NY : 2 * NY] = low

            def tree(x, width):
                if width == 1:
                    return leaf(x)
                left = tree(x, width // 2)
                right = tree(x + width // 2, width // 2)
                start = {2: 0, 4: 8, 8: 12, 16: 14}[width]
                put(start + x // width, left - right)
                return left + right

            put(XL - 1, tree(0, XL))

    def product(s):
        to = outs[s - 1] if s else own_ref
        for i in range(PART // 256):
            g = g_ref[s * PART + i * 256 : s * PART + (i + 1) * 256, :]
            u = lax.dot_general(
                sy_ref[...],
                g,
                (((1,), (1,)), ((), ())),
                preferred_element_type=jnp.float32,
            )
            high, low = split(u, 2)
            to[:, i * 256 : (i + 1) * 256] = high
            to[:, PART + i * 256 : PART + (i + 1) * 256] = low

    copy = pltpu.make_async_copy(own_ref, far_ref.at[0], sem)
    for s in range(STA):
        field(s)
        if s:
            product(s - 1)
        if s == 1:
            copy.start()
    product(STA - 1)
    copy.wait()


def message_kernel(code_ref, far_ref, *refs):
    u_refs = refs[: STA - 1]
    kept_ref, dest_ref, sx_ref, out_ref, coarse_ref, fine_ref, spot_ref, scale_ref, near_ref, sem = refs[STA - 1 :]
    copy = pltpu.make_async_copy(far_ref.at[0], near_ref, sem)
    copy.start()
    index_kernel(kept_ref, dest_ref, sx_ref, coarse_ref, fine_ref, spot_ref, scale_ref)
    low_half = iota((16, 128), 1) < NZ
    column_id = iota((16, 256), 1)
    groups = SLABS // 2

    def rows_of(g, t):
        return slice(t * (NY // 2) + g * 16, t * (NY // 2) + g * 16 + 16)

    def known(g):
        code = code_ref[2 * g : 2 * g + 2].reshape(16, 128)
        wide = jnp.concatenate([code, code], axis=1)
        return code, jnp.where(wide >= 0, wide & 511, -1)

    def picked(g, tables, base):
        pick = jnp.where(known(g)[1] == column_id + base, 1.0, 0.0).astype(jnp.bfloat16)
        total = None
        for part in (0, PART):
            both = []
            for t in (0, 1):
                both.append(
                    jnp.concatenate(
                        [u[rows_of(g, t), part + q * 128 : part + (q + 1) * 128] for u in tables for q in range(XL // 2)],
                        axis=0,
                    )
                )
            got = jnp.dot(pick, jnp.concatenate(both, axis=1), preferred_element_type=jnp.float32)
            total = got if total is None else total + got
        return total

    def coarse(g, s, u):
        lanes = PART - 128
        v = []
        for t in (0, 1):
            high = u[rows_of(g, t), lanes : lanes + 128].astype(jnp.float32)
            v.append(high + u[rows_of(g, t), PART + lanes : PART + lanes + 128].astype(jnp.float32))
        row = jnp.where(low_half, pltpu.roll(v[0], NZ, 1), v[1])
        out_ref[2 * g : 2 * g + 2, s * HALF : (s + 1) * HALF, :] = row.reshape(2, HALF, 128)

    got = [picked(g, u_refs[1:], 256) for g in range(groups)]
    for g in range(groups):
        for s in range(1, STA):
            coarse(g, s, u_refs[s - 1])
    copy.wait()
    for g in range(groups):
        coarse(g, 0, near_ref)
        both = got[g] + picked(g, (near_ref, u_refs[0]), 0)
        v0, v1 = both[:, :128], both[:, 128:]
        even = jnp.where(low_half, v0, pltpu.roll(v1, NZ, 1))
        odd = jnp.where(low_half, pltpu.roll(v0, NZ, 1), v1)
        fine = jnp.where(known(g)[0] >= 512, odd, even)
        out_ref[2 * g : 2 * g + 2, COARSE:MSG, :] = fine.reshape(2, FINE, 128)


def power(level_top, value):
    out = jnp.full(value.shape, 2.0 ** (-level_top / 2), jnp.float32)
    for level in range(1, level_top):
        out = jnp.where(value >= (1 << level), np.float32(2.0 ** (-(level_top - level) / 2)), out)
    return out


def index_kernel(kept_ref, dest_ref, sx_ref, coarse_ref, fine_ref, spot_ref, scale_ref):
    k = column(kept_ref[...].astype(jnp.float32)).astype(jnp.int32)
    a, pair, xs, _ = places_of(k)
    rank = earlier(xs.astype(jnp.float32)).astype(jnp.int32)
    one_a = jnp.where(iota((ROWS, SLABS), 1) == a, 1.0, 0.0).astype(jnp.bfloat16)
    sign = jnp.dot(one_a, sx_ref[...], preferred_element_type=jnp.float32)
    mine = station_col() * HALF + pair
    there = (iota((ROWS, SLABS * COARSE), 1) & (COARSE - 1)) == mine
    coarse_ref[...] = jnp.where(there, sign, 0.0).astype(jnp.bfloat16)
    key = jnp.where(xs < SLABS, xs * FINE + rank, -1)
    fine_ref[...] = jnp.where(iota((ROWS, SLABS * FINE), 1) == key, 1.0, 0.0).astype(jnp.bfloat16)
    dest = column(dest_ref[...].astype(jnp.float32))
    spot = turned(earlier(dest) * float(OWNERS) + dest).astype(jnp.int32)
    where = jnp.broadcast_to(spot, (OWNERS * CAP, ROWS)) == iota((OWNERS * CAP, ROWS), 0)
    spot_ref[...] = jnp.where(where, 1.0, 0.0).astype(jnp.bfloat16)
    b = 2 * (slab_pos() * HALF + pair)
    rowscale = power(8, a) * power(8, b)
    lanescale = power(6, iota((ROWS, LANES), 1) & (NZ - 1))
    scale_ref[...] = rowscale * lanescale


def dots(pick, parts):
    total = jnp.dot(pick, parts[0], preferred_element_type=jnp.float32)
    for part in parts[1:]:
        total = total + jnp.dot(pick, part, preferred_element_type=jnp.float32)
    return total


def combine_kernel(got_ref, coarse_ref, fine_ref, spot_ref, scale_ref, sz_ref, out_ref):
    coarse = got_ref[:, 0:COARSE, :].reshape(SLABS * COARSE, LANES)
    fine = got_ref[:, COARSE:MSG, :].reshape(SLABS * FINE, LANES)
    value = dots(coarse_ref[...], split(coarse, 3)) + dots(fine_ref[...], split(fine, 3))
    value = jnp.dot(jnp.concatenate(split(value, 3), axis=1), sz_ref[...], preferred_element_type=jnp.float32)
    value = value * scale_ref[...]
    placed = dots(spot_ref[...], split(value, 3))
    for slot in range(CAP):
        rows = placed[slot * OWNERS : (slot + 1) * OWNERS]
        out_ref[:, :, slot * LANES : (slot + 1) * LANES] = rows.reshape(OWNERS, 1, LANES)


VMEM = pl.BlockSpec(memory_space=pltpu.VMEM)
HBM = pl.BlockSpec(memory_space=pltpu.HBM)


def finish_kernel(got_ref, out_ref):
    for slot in range(CAP):
        out_ref[slot] = got_ref[:, :, slot * LANES : (slot + 1) * LANES].reshape(OWNERS, LANES)


def run(body, args, ins, shapes, outs, scratch=(), cost=None, limit=16 * MIB):
    return pl.pallas_call(
        body,
        out_shape=shapes,
        in_specs=ins,
        out_specs=outs,
        scratch_shapes=list(scratch),
        compiler_params=pltpu.CompilerParams(vmem_limit_bytes=limit),
        cost_estimate=cost,
    )(*args)


def struct(shape, dtype=jnp.float32):
    return jax.ShapeDtypeStruct(shape, dtype)


def lists(kept):
    cost = pl.CostEstimate(flops=3 * 10**10, bytes_accessed=MIB, transcendentals=0)
    return run(list_kernel, (kept,), [VMEM], struct((SLABS, FINE, 128), jnp.int32), VMEM, (), cost)


def tables(place, height, weight):
    cost = pl.CostEstimate(flops=2 * 512 * 256 * 4096, bytes_accessed=6 * MIB, transcendentals=1 << 20)
    part = struct((NY, 2 * PART), jnp.bfloat16)
    return run(
        table_kernel,
        (place.T, height.reshape(1, STA), jnp.transpose(weight, (0, 2, 1))),
        [VMEM, VMEM, HBM],
        [struct((FAR, NY, 2 * PART), jnp.bfloat16)] + [part] * (STA - 1),
        [HBM] + [VMEM] * (STA - 1),
        [
            pltpu.VMEM((XL, NZ, NY), jnp.float32),
            pltpu.VMEM((XL, NZ, NY), jnp.float32),
            pltpu.VMEM((NY, 2 * NY), jnp.bfloat16),
            pltpu.VMEM((TABS * NZ, 2 * NY), jnp.bfloat16),
            pltpu.VMEM((NY, 2 * PART), jnp.bfloat16),
            pltpu.SemaphoreType.DMA((NZ // 16,)),
            pltpu.SemaphoreType.DMA,
        ],
        cost,
        GRANT,
    )


def messages(codes, u, kept, dest, sx):
    bf = jnp.bfloat16
    outs = [
        struct((SLABS, MSG, LANES)),
        struct((ROWS, SLABS * COARSE), bf),
        struct((ROWS, SLABS * FINE), bf),
        struct((OWNERS * CAP, ROWS), bf),
        struct((ROWS, LANES)),
    ]
    return run(
        message_kernel,
        (codes, *u, kept, dest, sx),
        [VMEM, HBM] + [VMEM] * (STA + 2),
        outs,
        [VMEM] * 5,
        [pltpu.VMEM((NY, 2 * PART), bf), pltpu.SemaphoreType.DMA],
        None,
        44 * MIB,
    )


def combined(got, index, sz):
    return run(combine_kernel, (got, *index, sz), [VMEM] * 6, struct((OWNERS, 1, CAP * LANES)), VMEM)


def local(station_place, station_height, cell_weight, kept, dest):
    sz, sx = (jnp.asarray(c) for c in constants())
    kept = kept.reshape(STA, KEEP)
    dest = dest.reshape(STA, KEEP)
    codes = lax.all_to_all(lists(kept), "slab", 0, 0, tiled=True)
    u = tables(station_place, station_height, cell_weight)
    rows, *index = messages(codes, u, kept, dest, sx)
    got = lax.all_to_all(rows, "slab", 0, 0, tiled=True)
    out = lax.all_to_all(combined(got, index, sz), "sta", 0, 0, tiled=True)
    out = run(finish_kernel, (out,), [VMEM], struct((CAP, OWNERS, LANES)), VMEM)
    return jnp.transpose(out, (1, 0, 2))[None, None]


def solution(mesh):
    placed = (
        P("sta", None),
        P("sta"),
        P("slab", None, None),
        P("slab", "sta", None),
        P("slab", "sta", None, None),
    )
    return jax.shard_map(
        local,
        mesh=mesh,
        in_specs=placed,
        out_specs=P("slab", "sta", None, None, None),
        check_vma=False,
    )
```

```python
import jax
import jax.numpy as jnp
import numpy as np
from jax import lax
from jax.experimental import pallas as pl
from jax.experimental.pallas import tpu as pltpu
from jax.sharding import PartitionSpec as P

SCALE = 32.0
SLABS = 16
OWNERS = 32
STA = 4
KEEP = 16
ROWS = STA * KEEP
XL = 16
NX = 256
NY = 256
NZ = 64
HALF = 8
CAP = 6
FINE = 8
COARSE = STA * HALF
MSG = COARSE + FINE
LANES = 2 * NZ
TABS = STA * XL
MIB = 1 << 20
GRANT = 52000 << 10
FAR = 30


def signs(order):
    out = np.zeros((order, order), np.float32)
    out[0] = 1
    count = 1
    while count < order:
        width = order // count
        for k in range(count):
            out[count + k, k * width : k * width + width // 2] = 1
            out[count + k, k * width + width // 2 : (k + 1) * width] = -1
        count *= 2
    return out


def constants():
    sz = np.zeros((LANES, LANES), np.float32)
    sz[:NZ, :NZ] = signs(NZ).T
    sz[NZ:, NZ:] = signs(NZ).T
    sz = np.concatenate([sz] * 3, axis=0)
    sx = np.repeat(signs(SLABS), COARSE, axis=1)
    bf = jnp.bfloat16
    return np.asarray(sz, bf), np.asarray(sx, bf)


def slab_pos():
    return lax.axis_index("slab")


def iota(shape, dim):
    return lax.broadcasted_iota(jnp.int32, shape, dim)


def column(tile):
    eye = iota((KEEP, KEEP), 0) == iota((KEEP, KEEP), 1)
    parts = []
    for s in range(STA):
        row = jnp.broadcast_to(tile[s : s + 1, :], (KEEP, KEEP))
        parts.append(jnp.sum(jnp.where(eye, row, 0.0), axis=1, keepdims=True))
    return jnp.concatenate(parts, axis=0)


def turned(col):
    eye = iota((ROWS, ROWS), 0) == iota((ROWS, ROWS), 1)
    wide = jnp.broadcast_to(col, (ROWS, ROWS))
    return jnp.sum(jnp.where(eye, wide, 0.0), axis=0, keepdims=True)


def earlier(col):
    row = turned(col)
    before = iota((ROWS, ROWS), 1) < iota((ROWS, ROWS), 0)
    same = (jnp.broadcast_to(row, (ROWS, ROWS)) == jnp.broadcast_to(col, (ROWS, ROWS))) & before
    return jnp.sum(jnp.where(same, 1.0, 0.0), axis=1, keepdims=True)


def split(x, parts):
    out = []
    for i in range(parts):
        piece = x.astype(jnp.bfloat16)
        out.append(piece)
        if i + 1 < parts:
            x = x - piece.astype(jnp.float32)
    return out


def places_of(k):
    a = lax.shift_right_logical(k, 3)
    pair = k & (HALF - 1)
    xs = jnp.full_like(a, SLABS)
    tab = jnp.full_like(a, XL - 1)
    for least, shift, base in ((16, 0, 14), (32, 1, 12), (64, 2, 8), (128, 3, 0)):
        inside = a >= least
        off = a - least
        xs = jnp.where(inside, lax.shift_right_logical(off, shift), xs)
        tab = jnp.where(inside, base + (off & ((1 << shift) - 1)), tab)
    return a, pair, xs, tab


def station_col():
    return lax.shift_right_logical(iota((ROWS, 1), 0), 4)


def list_kernel(kept_ref, out_ref):
    k = column(kept_ref[...].astype(jnp.float32)).astype(jnp.int32)
    _, pair, xs, tab = places_of(k)
    table = station_col() * XL + tab
    row = (slab_pos() & 1) * HALF + pair
    code = (table & 1) * (16 * TABS // 2) + lax.shift_right_logical(table, 1) * 16 + row
    rank = earlier(xs.astype(jnp.float32)).astype(jnp.int32)
    key = turned((xs * FINE + rank).astype(jnp.float32)).astype(jnp.int32)
    coderow = turned(code.astype(jnp.float32))
    count = SLABS * FINE
    hit = jnp.broadcast_to(key, (count, ROWS)) == iota((count, ROWS), 0)
    found = jnp.sum(jnp.where(hit, jnp.broadcast_to(coderow, (count, ROWS)) + 1.0, 0.0), axis=1, keepdims=True)
    tile = jnp.broadcast_to(found - 1.0, (count, 128)).astype(jnp.int32)
    out_ref[...] = tile.reshape(SLABS, FINE, 128)


PART = XL * NZ


def haar_signs():
    row = iota((NY, 1), 0)
    b = 2 * (row & (NY // 2 - 1)) + lax.shift_right_logical(row, 7)
    start = jnp.zeros_like(b)
    width = jnp.full_like(b, NY)
    for level in range(1, 8):
        inside = b >= (1 << level)
        width = jnp.where(inside, NY >> level, width)
        start = jnp.where(inside, (b - (1 << level)) * (NY >> level), start)
    middle = jnp.where(b == 0, start + width, start + lax.shift_right_logical(width, 1))
    y = iota((NY, NY), 1)
    signed = jnp.where(y < middle, 1.0, jnp.where(y < start + width, -1.0, 0.0))
    signed = jnp.where(y < start, 0.0, signed).astype(jnp.bfloat16)
    return jnp.concatenate([signed, signed], axis=1)


def table_kernel(place_ref, height_ref, w_hbm, far_ref, *refs):
    outs = refs[: STA - 1]
    w_ref, ready_ref, sy_ref, g_ref, own_ref, w_sems, sem = refs[STA - 1 :]
    first = (slab_pos() * XL).astype(jnp.float32)
    yy = iota((1, NY), 1).astype(jnp.float32) + 0.5
    rows = 16
    arrivals = []
    for i in range(NZ // rows):
        at = (slice(None), pl.ds(i * rows, rows))
        arrivals.append(pltpu.make_async_copy(w_hbm.at[at], w_ref.at[at], w_sems.at[i]))
        arrivals[-1].start()
    sy_ref[...] = haar_signs()

    def field(s):
        east0 = place_ref[0:1, s : s + 1] * float(NX)
        north2 = (yy - place_ref[1:2, s : s + 1] * float(NY)) ** 2
        height = height_ref[0:1, s : s + 1]

        def cells(x, z0):
            zz = (z0 + iota((rows, 1), 0)).astype(jnp.float32) + 0.5 + height
            east = (first + (x + 0.5)) - east0
            r = lax.rsqrt((north2 + zz * zz) + east * east)
            return jnp.broadcast_to(SCALE * zz, (rows, NY)) * (r * r * r)

        if s == 0:
            for z0 in range(0, NZ, rows):
                for x in range(XL):
                    ready_ref[x, z0 : z0 + rows, :] = cells(x, z0)
        for z0 in range(0, NZ, rows):
            if s == 0:
                arrivals[z0 // rows].wait()

            def leaf(x):
                known = ready_ref[x, z0 : z0 + rows, :] if s == 0 else cells(x, z0)
                return w_ref[x, z0 : z0 + rows, :] * known

            def put(tab, value):
                at = slice((s * XL + tab) * NZ + z0, (s * XL + tab) * NZ + z0 + rows)
                high, low = split(value, 2)
                g_ref[at, 0:NY] = high
                g_ref[at, NY : 2 * NY] = low

            def tree(x, width):
                if width == 1:
                    return leaf(x)
                left = tree(x, width // 2)
                right = tree(x + width // 2, width // 2)
                start = {2: 0, 4: 8, 8: 12, 16: 14}[width]
                put(start + x // width, left - right)
                return left + right

            put(XL - 1, tree(0, XL))

    def product(s):
        to = outs[s - 1] if s else own_ref
        for i in range(PART // 256):
            g = g_ref[s * PART + i * 256 : s * PART + (i + 1) * 256, :]
            u = lax.dot_general(
                sy_ref[...],
                g,
                (((1,), (1,)), ((), ())),
                preferred_element_type=jnp.float32,
            )
            high, low = split(u, 2)
            to[:, i * 256 : (i + 1) * 256] = high
            to[:, PART + i * 256 : PART + (i + 1) * 256] = low

    copy = pltpu.make_async_copy(own_ref, far_ref.at[0], sem)
    for s in range(STA):
        field(s)
        if s:
            product(s - 1)
        if s == 1:
            copy.start()
    product(STA - 1)
    copy.wait()


def message_kernel(code_ref, far_ref, *refs):
    u_refs = refs[: STA - 1]
    kept_ref, dest_ref, sx_ref, out_ref, coarse_ref, fine_ref, spot_ref, scale_ref, near_ref, sem = refs[STA - 1 :]
    copy = pltpu.make_async_copy(far_ref.at[0], near_ref, sem)
    copy.start()
    index_kernel(kept_ref, dest_ref, sx_ref, coarse_ref, fine_ref, spot_ref, scale_ref)
    low_half = iota((16, 128), 1) < NZ
    groups = SLABS // 2

    def rows_of(g, t):
        return slice(t * (NY // 2) + g * 16, t * (NY // 2) + g * 16 + 16)

    def known(g):
        code = code_ref[2 * g : 2 * g + 2].reshape(16, 128)
        return code, jnp.where(code >= 0, code & 511, -1)

    def picked(g, tables, base):
        wide = jnp.concatenate([known(g)[1]] * len(tables), axis=1)
        pick = jnp.where(wide == iota(wide.shape, 1) + base, 1.0, 0.0).astype(jnp.bfloat16)
        total = None
        for part in (0, PART):
            both = []
            for t in (0, 1):
                both.append(
                    jnp.concatenate(
                        [u[rows_of(g, t), part + q * 128 : part + (q + 1) * 128] for u in tables for q in range(XL // 2)],
                        axis=0,
                    )
                )
            got = jnp.dot(pick, jnp.concatenate(both, axis=1), preferred_element_type=jnp.float32)
            total = got if total is None else total + got
        return total

    def coarse(g, s, u):
        lanes = PART - 128
        v = []
        for t in (0, 1):
            high = u[rows_of(g, t), lanes : lanes + 128].astype(jnp.float32)
            v.append(high + u[rows_of(g, t), PART + lanes : PART + lanes + 128].astype(jnp.float32))
        row = jnp.where(low_half, pltpu.roll(v[0], NZ, 1), v[1])
        out_ref[2 * g : 2 * g + 2, s * HALF : (s + 1) * HALF, :] = row.reshape(2, HALF, 128)

    got = [picked(g, u_refs[1:], 256) + picked(g, u_refs[:1], 128) for g in range(groups)]
    for g in range(groups):
        for s in range(1, STA):
            coarse(g, s, u_refs[s - 1])
    copy.wait()
    for g in range(groups):
        coarse(g, 0, near_ref)
        both = got[g] + picked(g, (near_ref,), 0)
        v0, v1 = both[:, :128], both[:, 128:]
        even = jnp.where(low_half, v0, pltpu.roll(v1, NZ, 1))
        odd = jnp.where(low_half, pltpu.roll(v0, NZ, 1), v1)
        fine = jnp.where(known(g)[0] >= 512, odd, even)
        out_ref[2 * g : 2 * g + 2, COARSE:MSG, :] = fine.reshape(2, FINE, 128)


def power(level_top, value):
    out = jnp.full(value.shape, 2.0 ** (-level_top / 2), jnp.float32)
    for level in range(1, level_top):
        out = jnp.where(value >= (1 << level), np.float32(2.0 ** (-(level_top - level) / 2)), out)
    return out


def index_kernel(kept_ref, dest_ref, sx_ref, coarse_ref, fine_ref, spot_ref, scale_ref):
    k = column(kept_ref[...].astype(jnp.float32)).astype(jnp.int32)
    a, pair, xs, _ = places_of(k)
    rank = earlier(xs.astype(jnp.float32)).astype(jnp.int32)
    one_a = jnp.where(iota((ROWS, SLABS), 1) == a, 1.0, 0.0).astype(jnp.bfloat16)
    sign = jnp.dot(one_a, sx_ref[...], preferred_element_type=jnp.float32)
    mine = station_col() * HALF + pair
    there = (iota((ROWS, SLABS * COARSE), 1) & (COARSE - 1)) == mine
    coarse_ref[...] = jnp.where(there, sign, 0.0).astype(jnp.bfloat16)
    key = jnp.where(xs < SLABS, xs * FINE + rank, -1)
    fine_ref[...] = jnp.where(iota((ROWS, SLABS * FINE), 1) == key, 1.0, 0.0).astype(jnp.bfloat16)
    dest = column(dest_ref[...].astype(jnp.float32))
    spot = turned(earlier(dest) * float(OWNERS) + dest).astype(jnp.int32)
    where = jnp.broadcast_to(spot, (OWNERS * CAP, ROWS)) == iota((OWNERS * CAP, ROWS), 0)
    spot_ref[...] = jnp.where(where, 1.0, 0.0).astype(jnp.bfloat16)
    b = 2 * (slab_pos() * HALF + pair)
    rowscale = power(8, a) * power(8, b)
    lanescale = power(6, iota((ROWS, LANES), 1) & (NZ - 1))
    scale_ref[...] = rowscale * lanescale


def dots(pick, parts):
    total = jnp.dot(pick, parts[0], preferred_element_type=jnp.float32)
    for part in parts[1:]:
        total = total + jnp.dot(pick, part, preferred_element_type=jnp.float32)
    return total


def combine_kernel(got_ref, coarse_ref, fine_ref, spot_ref, scale_ref, sz_ref, out_ref):
    coarse = got_ref[:, 0:COARSE, :].reshape(SLABS * COARSE, LANES)
    fine = got_ref[:, COARSE:MSG, :].reshape(SLABS * FINE, LANES)
    value = dots(coarse_ref[...], split(coarse, 3)) + dots(fine_ref[...], split(fine, 3))
    value = jnp.dot(jnp.concatenate(split(value, 3), axis=1), sz_ref[...], preferred_element_type=jnp.float32)
    value = value * scale_ref[...]
    placed = dots(spot_ref[...], split(value, 3))
    for slot in range(CAP):
        rows = placed[slot * OWNERS : (slot + 1) * OWNERS]
        out_ref[:, :, slot * LANES : (slot + 1) * LANES] = rows.reshape(OWNERS, 1, LANES)


VMEM = pl.BlockSpec(memory_space=pltpu.VMEM)
HBM = pl.BlockSpec(memory_space=pltpu.HBM)


def finish_kernel(got_ref, out_ref):
    for slot in range(CAP):
        out_ref[slot] = got_ref[:, :, slot * LANES : (slot + 1) * LANES].reshape(OWNERS, LANES)


def run(body, args, ins, shapes, outs, scratch=(), cost=None, limit=16 * MIB):
    return pl.pallas_call(
        body,
        out_shape=shapes,
        in_specs=ins,
        out_specs=outs,
        scratch_shapes=list(scratch),
        compiler_params=pltpu.CompilerParams(vmem_limit_bytes=limit),
        cost_estimate=cost,
    )(*args)


def struct(shape, dtype=jnp.float32):
    return jax.ShapeDtypeStruct(shape, dtype)


def lists(kept):
    cost = pl.CostEstimate(flops=3 * 10**10, bytes_accessed=MIB, transcendentals=0)
    return run(list_kernel, (kept,), [VMEM], struct((SLABS, FINE, 128), jnp.int32), VMEM, (), cost)


def tables(place, height, weight):
    cost = pl.CostEstimate(flops=2 * 512 * 256 * 4096, bytes_accessed=6 * MIB, transcendentals=1 << 20)
    part = struct((NY, 2 * PART), jnp.bfloat16)
    return run(
        table_kernel,
        (place.T, height.reshape(1, STA), jnp.transpose(weight, (0, 2, 1))),
        [VMEM, VMEM, HBM],
        [struct((FAR, NY, 2 * PART), jnp.bfloat16)] + [part] * (STA - 1),
        [HBM] + [VMEM] * (STA - 1),
        [
            pltpu.VMEM((XL, NZ, NY), jnp.float32),
            pltpu.VMEM((XL, NZ, NY), jnp.float32),
            pltpu.VMEM((NY, 2 * NY), jnp.bfloat16),
            pltpu.VMEM((TABS * NZ, 2 * NY), jnp.bfloat16),
            pltpu.VMEM((NY, 2 * PART), jnp.bfloat16),
            pltpu.SemaphoreType.DMA((NZ // 16,)),
            pltpu.SemaphoreType.DMA,
        ],
        cost,
        GRANT,
    )


def messages(codes, u, kept, dest, sx):
    bf = jnp.bfloat16
    outs = [
        struct((SLABS, MSG, LANES)),
        struct((ROWS, SLABS * COARSE), bf),
        struct((ROWS, SLABS * FINE), bf),
        struct((OWNERS * CAP, ROWS), bf),
        struct((ROWS, LANES)),
    ]
    return run(
        message_kernel,
        (codes, *u, kept, dest, sx),
        [VMEM, HBM] + [VMEM] * (STA + 2),
        outs,
        [VMEM] * 5,
        [pltpu.VMEM((NY, 2 * PART), bf), pltpu.SemaphoreType.DMA],
        None,
        44 * MIB,
    )


def combined(got, index, sz):
    return run(combine_kernel, (got, *index, sz), [VMEM] * 6, struct((OWNERS, 1, CAP * LANES)), VMEM)


def local(station_place, station_height, cell_weight, kept, dest):
    sz, sx = (jnp.asarray(c) for c in constants())
    kept = kept.reshape(STA, KEEP)
    dest = dest.reshape(STA, KEEP)
    codes = lax.all_to_all(lists(kept), "slab", 0, 0, tiled=True)
    u = tables(station_place, station_height, cell_weight)
    rows, *index = messages(codes, u, kept, dest, sx)
    got = lax.all_to_all(rows, "slab", 0, 0, tiled=True)
    out = lax.all_to_all(combined(got, index, sz), "sta", 0, 0, tiled=True)
    out = run(finish_kernel, (out,), [VMEM], struct((CAP, OWNERS, LANES)), VMEM)
    return jnp.transpose(out, (1, 0, 2))[None, None]


def solution(mesh):
    placed = (
        P("sta", None),
        P("sta"),
        P("slab", None, None),
        P("slab", "sta", None),
        P("slab", "sta", None, None),
    )
    return jax.shard_map(
        local,
        mesh=mesh,
        in_specs=placed,
        out_specs=P("slab", "sta", None, None, None),
        check_vma=False,
    )
```
